32 devices in a mesh: grp: 16 (over z, x, core), dist: 2 (over y).
Axes of the slice: x: 2, y: 2, z: 4, core: 2. Of those that a mesh axis runs over, the one named last changes fastest.
Arguments:
- orbitals: bfloat16 [16, 64, 4096], P('grp', 'dist'), may hold values from -6 to 6
- occupations: bfloat16 [16], P('grp'), may hold values from 0.19921875 to 1
Outputs:
- exchange_action: float32 [16, 64, 4096], P('grp', 'dist')
The draws below stay inside these ranges and needn't reach their ends.
All inputs are finite; a program needn't handle non-finite values.
Results may differ from the reference program's by a relative error of at most 0.0003.
Values may be sent and summed in bfloat16 or wider, within the bound.
A program may use at most 64 MiB of HBM per device.

```python
import math
import jax
import jax.numpy as jnp
from jax import lax

GRID = 64
ORBITALS = 16


def block_levels(own_key, shape, pieces, least, largest):
    level, own = 1.0, jax.random.fold_in(own_key, 6)
    for dim, blocks in pieces:
        steps = jnp.exp(jax.random.uniform(jax.random.fold_in(own, dim), (blocks,), jnp.float32, least / len(pieces), largest / len(pieces)))
        level = level * jnp.repeat(steps, shape[dim] // blocks).reshape([-1 if axis == dim else 1 for axis in range(len(shape))])
    return level


def scatter_about(rng, dims, scale, limit, shards=(), held_as=jnp.bfloat16):
    drawn = jax.random.normal(rng, dims, jnp.float32) * scale
    if len(shards) > 0:
        drawn = block_levels(rng, dims, shards, -0.22, 0.18) * drawn
    return jnp.clip(drawn, min=-limit, max=limit).astype(held_as)


def setup_inputs(seed: int = 0) -> dict:
    keys = jax.random.split(jax.random.key(seed), 3)
    orbitals = scatter_about(keys[0], (ORBITALS, GRID, GRID * GRID), 1.0, 6.0, ((0, 16), (1, 2)))
    occupations = jnp.clip(0.19921875 + 0.80078125 * jax.random.uniform(keys[1], (ORBITALS,), jnp.float32) ** block_levels(keys[1], (ORBITALS,), ((0, 16),), -0.2, 0.2), 0.19921875, 1.0).astype(jnp.bfloat16)
    return dict(orbitals=orbitals, occupations=occupations)


box_length = 7.0


def reference(orbitals, occupations):
    orbital_count = orbitals.shape[0]
    points = GRID
    fields = orbitals.astype(jnp.float32).reshape(orbital_count, points, points, points)
    weights = occupations.astype(jnp.float32)
    position = jnp.arange(points)
    folded = jnp.minimum(position, points - position).astype(jnp.float32)
    halfway = jnp.arange(points // 2 + 1).astype(jnp.float32)
    squares = folded[:, None, None] ** 2 + folded[None, :, None] ** 2 + halfway[None, None, :] ** 2
    scale = (2.0 * math.pi / box_length) ** 2
    kernel = jnp.where(squares > 0.5, 4.0 * math.pi / (scale * jnp.maximum(squares, 1.0)), 0.0)

    def poisson_solve(density):
        spectrum = jnp.fft.rfftn(density, axes=(1, 2, 3))
        return jnp.fft.irfftn(spectrum * kernel, s=(points, points, points), axes=(1, 2, 3))

    def add_distance(offset, summed):
        partner = jnp.roll(fields, -offset, axis=0)
        partner_weight = jnp.roll(weights, -offset)
        potential = poisson_solve(fields * partner)
        toward = potential * partner * partner_weight[:, None, None, None]
        reverse_weight = jnp.logical_and(offset > 0, 2 * offset < orbital_count).astype(jnp.float32)
        backward = potential * fields * (weights * reverse_weight)[:, None, None, None]
        return summed + toward + jnp.roll(backward, offset, axis=0)

    summed = lax.fori_loop(0, orbital_count // 2 + 1, add_distance, jnp.zeros_like(fields))
    return (-summed).reshape(orbital_count, points, points * points)
```

```python
import functools
import math

import jax
import jax.numpy as jnp
import numpy as np
from jax import lax
from jax.experimental import pallas as pl
from jax.experimental.pallas import tpu as pltpu
from jax.sharding import PartitionSpec as P

box_length = 7.0
bf16, f32 = jnp.bfloat16, jnp.float32


def cas_tables(points):
    position = np.arange(points)
    angle = (position[:, None] * position[None, :] % points) * (2.0 * math.pi / points)
    table = np.cos(angle) + np.sin(angle)
    high = table.astype(bf16)
    low = (table - high.astype(np.float64)).astype(bf16)
    high, low = high.astype(np.float32), low.astype(np.float32)
    left = np.block([[high, high], [low, low]])
    two = np.eye(2, dtype=np.float32)
    wide_high, wide_low = np.kron(two, high), np.kron(two, low)
    right = np.block([[wide_high, wide_low], [wide_high, wide_low]])
    return left.astype(bf16), right.astype(bf16)


def split(value):
    high = value.astype(bf16)
    low = (value - high.astype(f32)).astype(bf16)
    return high, low


def from_left(left, value):
    points = value.shape[0]
    both = jnp.dot(left, jnp.concatenate(split(value), axis=0), preferred_element_type=f32)
    return both[:points] + both[points:]


def from_right(right, value):
    width = value.shape[1]
    both = jnp.dot(jnp.concatenate(split(value), axis=1), right, preferred_element_type=f32)
    return both[:, :width] + both[:, width:]


def lower_lanes(shape):
    return lax.broadcasted_iota(jnp.int32, shape, 1) < shape[1] // 2


def interleave(first, second):
    width = first.shape[1]
    low = lower_lanes(first.shape)
    even = jnp.where(low, first, pltpu.roll(second, width // 2, 1))
    odd = jnp.where(low, pltpu.roll(first, width // 2, 1), second)
    return jnp.concatenate([even, odd], axis=1)


def fill_kernel(points, table_ref):
    coupling = box_length**2 / (math.pi * points**3)
    shape = (points, 2 * points)

    def squares(index):
        folded = jnp.minimum(index, points - index)
        return folded * folded

    rows = squares(lax.broadcasted_iota(jnp.int32, shape, 0))
    lanes = squares(lax.broadcasted_iota(jnp.int32, shape, 1) % points)

    def step(k, carry):
        total = (rows + lanes + squares(k)).astype(f32)
        value = jnp.where(total > 0.5, coupling / jnp.maximum(total, 1.0), 0.0)
        table_ref[pl.ds(pl.multiple_of(k * points, points), points), :] = value
        return carry

    lax.fori_loop(0, points, step, 0)


def fill_own(points, own_ref, twin_ref):
    width = 2 * points

    def step(y, carry):
        part = own_ref[:, pl.ds(pl.multiple_of(y * width, width), width)].astype(f32)
        twin_ref[:, pl.ds(pl.multiple_of(y * 2 * width, width), 2 * width)] = interleave(part, part)
        return carry

    lax.fori_loop(0, points // 2, step, 0)


def solve_pair(points, first_ref, second_ref, weights, left, right, twin_ref, pair_ref, field_ref, table_ref, sum_ref):
    width = 2 * points
    group = 8

    def into(y, carry):
        here = pl.ds(pl.multiple_of(y * width, width), width)
        there = pl.ds(pl.multiple_of(y * 2 * width, width), 2 * width)
        both = interleave(first_ref[:, here].astype(f32), second_ref[:, here].astype(f32))
        pair_ref[:, there] = both
        out = from_left(left, both * twin_ref[:, there])
        field_ref[pl.ds(2 * y, points, stride=points), :] = out[:, :width]
        field_ref[pl.ds(2 * y + 1, points, stride=points), :] = out[:, width:]
        return carry

    lax.fori_loop(0, points // 2, into, 0, unroll=4)

    def middle(x, carry):
        rows = group * points
        base = pl.multiple_of(x * rows, rows)
        parts = []
        for two in range(group // 2):
            at = base + two * 2 * points
            value = jnp.concatenate(
                [field_ref[pl.ds(at, points), :], field_ref[pl.ds(at + points, points), :]], axis=1
            )
            value = from_left(left, value)
            parts += [value[:, :width], value[:, width:]]
        value = from_right(right, jnp.concatenate(parts, axis=0))
        value = from_right(right, value * table_ref[pl.ds(base, rows), :])
        for two in range(group // 2):
            at = two * 2 * points
            part = jnp.concatenate([value[at : at + points], value[at + points : at + 2 * points]], axis=1)
            part = from_left(left, part)
            field_ref[pl.ds(base + at, points), :] = part[:, :width]
            field_ref[pl.ds(base + at + points, points), :] = part[:, width:]
        return carry

    lax.fori_loop(0, points // group, middle, 0)

    def out_of(y, carry):
        there = pl.ds(pl.multiple_of(y * 2 * width, width), 2 * width)
        value = jnp.concatenate(
            [
                field_ref[pl.ds(2 * y, points, stride=points), :],
                field_ref[pl.ds(2 * y + 1, points, stride=points), :],
            ],
            axis=1,
        )
        value = from_left(left, value)
        sum_ref[:, there] += value * (pair_ref[:, there] * weights)
        return carry

    lax.fori_loop(0, points // 2, out_of, 0, unroll=4)


def lane_weights(points, first, second):
    lane = lax.broadcasted_iota(jnp.int32, (1, 4 * points), 1) % (2 * points)
    return jnp.where(lane < points, first, second)


def folded_sum(points, sum_ref, y):
    width = 2 * points
    at = pl.multiple_of(y * 2 * width, width)
    even, odd = sum_ref[:, pl.ds(at, width)], sum_ref[:, pl.ds(at + width, width)]
    even = even + pltpu.roll(even, points, 1)
    odd = odd + pltpu.roll(odd, points, 1)
    return -jnp.where(lower_lanes(even.shape), even, odd)


def work(points, own_ref, visit_ref, weight_ref, left_ref, right_ref, out_ref, twin_ref, pair_ref, field_ref, table_ref, sum_ref):
    width = 2 * points
    fill_kernel(points, table_ref)
    fill_own(points, own_ref, twin_ref)
    sum_ref[...] = jnp.zeros_like(sum_ref)
    left, right = left_ref[...], right_ref[...]

    def pair(p, carry):
        weights = lane_weights(points, weight_ref[0, 2 * p], weight_ref[0, 2 * p + 1])
        solve_pair(
            points, visit_ref.at[2 * p], visit_ref.at[2 * p + 1], weights, left, right,
            twin_ref, pair_ref, field_ref, table_ref, sum_ref,
        )
        return carry

    lax.fori_loop(0, visit_ref.shape[0] // 2, pair, 0)

    def fold(y, carry):
        out_ref[:, pl.ds(pl.multiple_of(y * width, width), width)] = folded_sum(points, sum_ref, y)
        return carry

    lax.fori_loop(0, points // 2, fold, 0)


def act(own, visits, weights):
    points = own.shape[0]
    left, right = cas_tables(points)
    vmem = pl.BlockSpec(memory_space=pltpu.VMEM)
    wide = (points, 2 * points * points)
    tall = (points * points, 2 * points)
    return pl.pallas_call(
        functools.partial(work, points),
        out_shape=jax.ShapeDtypeStruct(own.shape, f32),
        in_specs=[vmem, vmem, pl.BlockSpec(memory_space=pltpu.SMEM), vmem, vmem],
        out_specs=vmem,
        scratch_shapes=[
            pltpu.VMEM(wide, f32),
            pltpu.VMEM(wide, f32),
            pltpu.VMEM(tall, f32),
            pltpu.VMEM(tall, f32),
            pltpu.VMEM(wide, f32),
        ],
        compiler_params=pltpu.CompilerParams(vmem_limit_bytes=48 * 2**20),
    )(own, visits, weights, jnp.asarray(left), jnp.asarray(right))


def body(orbitals, occupations):
    lanes = lax.axis_size("dist")
    lane = lax.axis_index("dist")
    own = lax.all_gather(orbitals, "dist", axis=1, tiled=True)[0]
    spread = lax.all_gather(orbitals, "grp", axis=0, tiled=True)
    spread_occ = lax.all_gather(occupations, "grp", axis=0, tiled=True)
    orbs, planes, area = spread.shape
    sorted_by_lane = spread.reshape(orbs // lanes, lanes, planes, area).swapaxes(0, 1)
    visits = lax.all_to_all(sorted_by_lane, "dist", split_axis=0, concat_axis=2, tiled=True)[0]
    mine = lax.dynamic_index_in_dim(spread_occ.reshape(orbs // lanes, lanes), lane, 1, keepdims=False)
    partial = act(own, visits, mine.astype(f32)[None])
    return lax.psum_scatter(partial, "dist", scatter_dimension=0, tiled=True)[None]


def solution(mesh):
    in_specs = (P("grp", "dist", None), P("grp"))
    out_specs = P("grp", "dist", None)
    return jax.shard_map(body, mesh=mesh, in_specs=in_specs, out_specs=out_specs, check_vma=False)
```

```python
import functools
import math

import jax
import jax.numpy as jnp
import numpy as np
from jax import lax
from jax.experimental import pallas as pl
from jax.experimental.pallas import tpu as pltpu
from jax.sharding import PartitionSpec as P

box_length = 7.0
bf16, f32 = jnp.bfloat16, jnp.float32


def cas_tables(points):
    position = np.arange(points)
    angle = (position[:, None] * position[None, :] % points) * (2.0 * math.pi / points)
    table = np.cos(angle) + np.sin(angle)
    high = table.astype(bf16)
    low = (table - high.astype(np.float64)).astype(bf16)
    high, low = high.astype(np.float32), low.astype(np.float32)
    left = np.block([[high, high], [low, low]])
    two = np.eye(2, dtype=np.float32)
    wide_high, wide_low = np.kron(two, high), np.kron(two, low)
    right = np.block([[wide_high, wide_low], [wide_high, wide_low]])
    return left.astype(bf16), right.astype(bf16)


def split(value):
    high = value.astype(bf16)
    low = (value - high.astype(f32)).astype(bf16)
    return high, low


def from_left(left, value):
    points = value.shape[0]
    both = jnp.dot(left, jnp.concatenate(split(value), axis=0), preferred_element_type=f32)
    return both[:points] + both[points:]


def from_right(right, value):
    width = value.shape[1]
    both = jnp.dot(jnp.concatenate(split(value), axis=1), right, preferred_element_type=f32)
    return both[:, :width] + both[:, width:]


def lower_lanes(shape):
    return lax.broadcasted_iota(jnp.int32, shape, 1) < shape[1] // 2


def interleave(first, second):
    width = first.shape[1]
    low = lower_lanes(first.shape)
    even = jnp.where(low, first, pltpu.roll(second, width // 2, 1))
    odd = jnp.where(low, pltpu.roll(first, width // 2, 1), second)
    return jnp.concatenate([even, odd], axis=1)


def fill_kernel(points, table_ref):
    coupling = box_length**2 / (math.pi * points**3)
    shape = (points, 2 * points)

    def squares(index):
        folded = jnp.minimum(index, points - index)
        return folded * folded

    rows = squares(lax.broadcasted_iota(jnp.int32, shape, 0))
    lanes = squares(lax.broadcasted_iota(jnp.int32, shape, 1) % points)

    def step(k, carry):
        total = (rows + lanes + squares(k)).astype(f32)
        value = jnp.where(total > 0.5, coupling / jnp.maximum(total, 1.0), 0.0)
        table_ref[pl.ds(pl.multiple_of(k * points, points), points), :] = value
        return carry

    lax.fori_loop(0, points, step, 0)


def fill_own(points, own_ref, twin_ref):
    width = 2 * points

    def step(y, carry):
        part = own_ref[:, pl.ds(pl.multiple_of(y * width, width), width)].astype(f32)
        twin_ref[:, pl.ds(pl.multiple_of(y * 2 * width, width), 2 * width)] = interleave(part, part)
        return carry

    lax.fori_loop(0, points // 2, step, 0)


def solve_pair(points, first_ref, second_ref, weights, left, right, twin_ref, pair_ref, field_ref, table_ref, sum_ref, between=None):
    width = 2 * points
    group = 8

    def into(y, carry):
        here = pl.ds(pl.multiple_of(y * width, width), width)
        there = pl.ds(pl.multiple_of(y * 2 * width, width), 2 * width)
        both = interleave(first_ref[:, here].astype(f32), second_ref[:, here].astype(f32))
        pair_ref[:, there] = both
        out = from_left(left, both * twin_ref[:, there])
        field_ref[pl.ds(2 * y, points, stride=points), :] = out[:, :width]
        field_ref[pl.ds(2 * y + 1, points, stride=points), :] = out[:, width:]
        return carry

    lax.fori_loop(0, points // 2, into, 0, unroll=4)

    def middle(x, carry):
        rows = group * points
        base = pl.multiple_of(x * rows, rows)
        parts = []
        for two in range(group // 2):
            at = base + two * 2 * points
            value = jnp.concatenate(
                [field_ref[pl.ds(at, points), :], field_ref[pl.ds(at + points, points), :]], axis=1
            )
            value = from_left(left, value)
            parts += [value[:, :width], value[:, width:]]
        value = from_right(right, jnp.concatenate(parts, axis=0))
        value = from_right(right, value * table_ref[pl.ds(base, rows), :])
        for two in range(group // 2):
            at = two * 2 * points
            part = jnp.concatenate([value[at : at + points], value[at + points : at + 2 * points]], axis=1)
            part = from_left(left, part)
            field_ref[pl.ds(base + at, points), :] = part[:, :width]
            field_ref[pl.ds(base + at + points, points), :] = part[:, width:]
        return carry

    lax.fori_loop(0, points // group, middle, 0)

    if between is not None:
        between()

    def out_of(y, carry):
        there = pl.ds(pl.multiple_of(y * 2 * width, width), 2 * width)
        value = jnp.concatenate(
            [
                field_ref[pl.ds(2 * y, points, stride=points), :],
                field_ref[pl.ds(2 * y + 1, points, stride=points), :],
            ],
            axis=1,
        )
        value = from_left(left, value)
        sum_ref[:, there] += value * (pair_ref[:, there] * weights)
        return carry

    lax.fori_loop(0, points // 2, out_of, 0, unroll=4)


def lane_weights(points, first, second):
    lane = lax.broadcasted_iota(jnp.int32, (1, 4 * points), 1) % (2 * points)
    return jnp.where(lane < points, first, second)


def folded_sum(points, sum_ref, y, rows=slice(None)):
    width = 2 * points
    at = pl.multiple_of(y * 2 * width, width)
    even, odd = sum_ref[rows, pl.ds(at, width)], sum_ref[rows, pl.ds(at + width, width)]
    even = even + pltpu.roll(even, points, 1)
    odd = odd + pltpu.roll(odd, points, 1)
    return -jnp.where(lower_lanes(even.shape), even, odd)


def work(points, own_ref, visit_ref, weight_ref, left_ref, right_ref, out_ref, twin_ref, pair_ref, field_ref, table_ref, sum_ref):
    width = 2 * points
    fill_kernel(points, table_ref)
    fill_own(points, own_ref, twin_ref)
    sum_ref[...] = jnp.zeros_like(sum_ref)
    left, right = left_ref[...], right_ref[...]

    def pair(p, carry):
        weights = lane_weights(points, weight_ref[0, 2 * p], weight_ref[0, 2 * p + 1])
        solve_pair(
            points, visit_ref.at[2 * p], visit_ref.at[2 * p + 1], weights, left, right,
            twin_ref, pair_ref, field_ref, table_ref, sum_ref,
        )
        return carry

    lax.fori_loop(0, visit_ref.shape[0] // 2, pair, 0)

    def fold(y, carry):
        out_ref[:, pl.ds(pl.multiple_of(y * width, width), width)] = folded_sum(points, sum_ref, y)
        return carry

    lax.fori_loop(0, points // 2, fold, 0)


def act(own, visits, weights):
    points = own.shape[0]
    left, right = cas_tables(points)
    vmem = pl.BlockSpec(memory_space=pltpu.VMEM)
    wide = (points, 2 * points * points)
    tall = (points * points, 2 * points)
    return pl.pallas_call(
        functools.partial(work, points),
        out_shape=jax.ShapeDtypeStruct(own.shape, f32),
        in_specs=[vmem, vmem, pl.BlockSpec(memory_space=pltpu.SMEM), vmem, vmem],
        out_specs=vmem,
        scratch_shapes=[
            pltpu.VMEM(wide, f32),
            pltpu.VMEM(wide, f32),
            pltpu.VMEM(tall, f32),
            pltpu.VMEM(tall, f32),
            pltpu.VMEM(wide, f32),
        ],
        compiler_params=pltpu.CompilerParams(vmem_limit_bytes=48 * 2**20),
    )(own, visits, weights, jnp.asarray(left), jnp.asarray(right))


def joint_work(
    points, chips, orb_ref, occ_ref, left_ref, right_ref, out_ref,
    own_ref, visit_ref, twin_ref, pair_ref, field_ref, table_ref, sum_ref, leave_ref, arrive_ref,
    ring_sent, ring_got, core_sent, core_got, lane_sent, lane_got, sum_sent, sum_got,
):
    planes, area = orb_ref.shape
    width = 2 * points
    rank, lane = lax.axis_index("grp"), lax.axis_index("dist")
    core, chip = rank % 2, rank // 2
    place = jnp.where(chip % 2 == 0, chip // 2, chips - 1 - chip // 2)

    def device_at(spot):
        spot = (spot + chips) % chips
        return jnp.where(spot < chips // 2, 2 * spot, 2 * (chips - 1 - spot) + 1) * 2 + core

    ahead = (device_at(place + 1 - 2 * core), lane)
    behind = (device_at(place - 1 + 2 * core), lane)
    sibling = (chip * 2 + 1 - core, lane)
    across = (rank, 1 - lane)
    most = chips // 2
    steps = most - core * (2 * most + 1 - chips)
    source = core == lane

    def rows_of(which):
        side = lane + which - 2 * lane * which
        return pl.ds(pl.multiple_of(side * planes, planes), planes)

    def ring_copy(step, which):
        held = jnp.where(step == 0, 0, 2 * step - 1 + core)
        return pltpu.make_async_remote_copy(
            src_ref=visit_ref.at[held, rows_of(which)],
            dst_ref=visit_ref.at[2 * step + 1 + core, rows_of(which)],
            send_sem=ring_sent.at[step, which],
            recv_sem=ring_got.at[step, which],
            device_id=ahead,
            device_id_type=pl.DeviceIdType.MESH,
        )

    def core_copy(slot, which):
        return pltpu.make_async_remote_copy(
            src_ref=visit_ref.at[slot, rows_of(which)],
            dst_ref=visit_ref.at[slot, rows_of(which)],
            send_sem=core_sent.at[slot, which],
            recv_sem=core_got.at[slot, which],
            device_id=sibling,
            device_id_type=pl.DeviceIdType.MESH,
        )

    lane_copy = pltpu.make_async_remote_copy(
        src_ref=own_ref.at[rows_of(0)],
        dst_ref=own_ref.at[rows_of(0)],
        send_sem=lane_sent,
        recv_sem=lane_got,
        device_id=across,
        device_id_type=pl.DeviceIdType.MESH,
    )
    chunks = sum_sent.shape[0]
    chunk = area // chunks

    def sum_copy(part):
        here = pl.ds(part * chunk, chunk)
        return pltpu.make_async_remote_copy(
            src_ref=leave_ref.at[:, here],
            dst_ref=arrive_ref.at[:, here],
            send_sem=sum_sent.at[part],
            recv_sem=sum_got.at[part],
            device_id=across,
            device_id_type=pl.DeviceIdType.MESH,
        )

    barrier = pltpu.get_barrier_semaphore()
    for other in (ahead, behind, sibling, across):
        pl.semaphore_signal(barrier, inc=1, device_id=other, device_id_type=pl.DeviceIdType.MESH)

    occupied = jnp.full((planes, width), occ_ref[0], f32).astype(bf16)
    own_ref[rows_of(0), pl.ds(0, area)] = orb_ref[...]
    own_ref[rows_of(0), pl.ds(area, width)] = occupied

    @pl.when(source)
    def _():
        visit_ref[0, rows_of(0), :] = own_ref[rows_of(0), :]

    pl.semaphore_wait(barrier, 4)
    lane_copy.start()

    @pl.when(source)
    def _():
        ring_copy(0, 0).start()
        core_copy(0, 0).start()

    fill_kernel(points, table_ref)
    sum_ref[...] = jnp.zeros_like(sum_ref)
    lane_copy.wait_recv()

    @pl.when(source)
    def _():
        visit_ref[0, rows_of(1), :] = own_ref[rows_of(1), :]
        ring_copy(0, 1).start()
        core_copy(0, 1).start()

    @pl.when(jnp.logical_not(source))
    def _():
        for which in range(2):
            core_copy(0, which).wait_recv()
            ring_copy(0, which).start()

    fill_own(points, own_ref, twin_ref)

    def service(step):
        @pl.when(step <= steps)
        def _():
            for which in range(2):
                ring_copy(step - 1, which).wait_recv()

                @pl.when(step < steps)
                def _():
                    ring_copy(step, which).start()

                core_copy(2 * step - 1 + core, which).start()

    service(1)
    left, right = left_ref[...], right_ref[...]
    pairs = chips // 2

    def pair(p, carry):
        @pl.when(core == 1)
        def _():
            for which in range(2):
                core_copy(2 * p + 1, which).wait_recv()

        @pl.when(jnp.logical_and(core == 0, p > 0))
        def _():
            for which in range(2):
                core_copy(2 * p, which).wait_recv()

        near = visit_ref[2 * p, pl.ds(0, 16), pl.ds(area, width)].astype(f32)[:1]
        far = visit_ref[2 * p + 1, pl.ds(0, 16), pl.ds(area, width)].astype(f32)[:1]
        weights = jnp.where(lower_lanes(near.shape), near, far)
        weights = jnp.concatenate([weights, weights], axis=1)
        solve_pair(
            points, visit_ref.at[2 * p], visit_ref.at[2 * p + 1], weights, left, right,
            twin_ref, pair_ref, field_ref, table_ref, sum_ref, lambda: service(p + 2),
        )
        return carry

    lax.fori_loop(0, pairs, pair, 0)

    share = points // 2 // chunks
    for part in range(chunks):

        def fold(y, carry):
            here = pl.ds(pl.multiple_of(y * width, width), width)
            leave_ref[:, here] = folded_sum(points, sum_ref, y, rows_of(1))
            return carry

        lax.fori_loop(part * share, (part + 1) * share, fold, 0)
        sum_copy(part).start()
    for part in range(chunks):
        sum_copy(part).wait_recv()

        def add(y, carry):
            here = pl.ds(pl.multiple_of(y * width, width), width)
            out_ref[:, here] = folded_sum(points, sum_ref, y, rows_of(0)) + arrive_ref[:, here]
            return carry

        lax.fori_loop(part * share, (part + 1) * share, add, 0)

    for part in range(chunks):
        sum_copy(part).wait_send()
    lane_copy.wait_send()
    for which in range(2):

        @pl.when(source)
        def _():
            core_copy(0, which).wait_send()

        for step in range(most):

            @pl.when(step < steps)
            def _():
                ring_copy(step, which).wait_send()
                core_copy(2 * step + 1 + core, which).wait_send()


def joint(orbitals, occupations):
    planes, area = orbitals.shape
    points = planes * lax.axis_size("dist")
    chips = lax.axis_size("grp") // 2
    left, right = cas_tables(points)
    vmem = pl.BlockSpec(memory_space=pltpu.VMEM)
    wide = (points, 2 * points * points)
    tall = (points * points, 2 * points)
    chunks = 4
    dma = pltpu.SemaphoreType.DMA
    return pl.pallas_call(
        functools.partial(joint_work, points, chips),
        out_shape=jax.ShapeDtypeStruct((planes, area), f32),
        in_specs=[vmem, pl.BlockSpec(memory_space=pltpu.SMEM), vmem, vmem],
        out_specs=vmem,
        scratch_shapes=[
            pltpu.VMEM((points, area + 2 * points), bf16),
            pltpu.VMEM((chips, points, area + 2 * points), bf16),
            pltpu.VMEM(wide, f32),
            pltpu.VMEM(wide, f32),
            pltpu.VMEM(tall, f32),
            pltpu.VMEM(tall, f32),
            pltpu.VMEM(wide, f32),
            pltpu.VMEM((planes, area), f32),
            pltpu.VMEM((planes, area), f32),
            dma((chips // 2, 2)),
            dma((chips // 2, 2)),
            dma((chips, 2)),
            dma((chips, 2)),
            dma,
            dma,
            dma((chunks,)),
            dma((chunks,)),
        ],
        compiler_params=pltpu.CompilerParams(
            vmem_limit_bytes=48 * 2**20, collective_id=0, has_side_effects=True
        ),
    )(orbitals, occupations.astype(f32), jnp.asarray(left), jnp.asarray(right))


def body(orbitals, occupations):
    lanes = lax.axis_size("dist")
    if lanes == 2 and orbitals.shape[0] == 1 and lax.axis_size("grp") % 4 == 0:
        return joint(orbitals[0], occupations)[None]
    lane = lax.axis_index("dist")
    own = lax.all_gather(orbitals, "dist", axis=1, tiled=True)[0]
    spread = lax.all_gather(orbitals, "grp", axis=0, tiled=True)
    spread_occ = lax.all_gather(occupations, "grp", axis=0, tiled=True)
    orbs, planes, area = spread.shape
    sorted_by_lane = spread.reshape(orbs // lanes, lanes, planes, area).swapaxes(0, 1)
    visits = lax.all_to_all(sorted_by_lane, "dist", split_axis=0, concat_axis=2, tiled=True)[0]
    mine = lax.dynamic_index_in_dim(spread_occ.reshape(orbs // lanes, lanes), lane, 1, keepdims=False)
    partial = act(own, visits, mine.astype(f32)[None])
    return lax.psum_scatter(partial, "dist", scatter_dimension=0, tiled=True)[None]


def solution(mesh):
    in_specs = (P("grp", "dist", None), P("grp"))
    out_specs = P("grp", "dist", None)
    return jax.shard_map(body, mesh=mesh, in_specs=in_specs, out_specs=out_specs, check_vma=False)
```

```python
import functools
import math

import jax
import jax.numpy as jnp
import numpy as np
from jax import lax
from jax.experimental import pallas as pl
from jax.experimental.pallas import tpu as pltpu
from jax.sharding import PartitionSpec as P

box_length = 7.0
bf16, f32 = jnp.bfloat16, jnp.float32


def cas_tables(points):
    position = np.arange(points)
    angle = (position[:, None] * position[None, :] % points) * (2.0 * math.pi / points)
    table = np.cos(angle) + np.sin(angle)
    high = table.astype(bf16)
    low = (table - high.astype(np.float64)).astype(bf16)
    high, low = high.astype(np.float32), low.astype(np.float32)
    left = np.block([[high, high], [low, low]])
    two = np.eye(2, dtype=np.float32)
    wide_high, wide_low = np.kron(two, high), np.kron(two, low)
    right = np.block([[wide_high, wide_low], [wide_high, wide_low]])
    return left.astype(bf16), right.astype(bf16)


def split(value):
    high = value.astype(bf16)
    low = (value - high.astype(f32)).astype(bf16)
    return high, low


def from_left(left, value):
    points = value.shape[0]
    both = jnp.dot(left, jnp.concatenate(split(value), axis=0), preferred_element_type=f32)
    return both[:points] + both[points:]


def from_right(right, value):
    width = value.shape[1]
    both = jnp.dot(jnp.concatenate(split(value), axis=1), right, preferred_element_type=f32)
    return both[:, :width] + both[:, width:]


def lower_lanes(shape):
    return lax.broadcasted_iota(jnp.int32, shape, 1) < shape[1] // 2


def interleave(first, second):
    width = first.shape[1]
    low = lower_lanes(first.shape)
    even = jnp.where(low, first, pltpu.roll(second, width // 2, 1))
    odd = jnp.where(low, pltpu.roll(first, width // 2, 1), second)
    return jnp.concatenate([even, odd], axis=1)


def fill_kernel(points, table_ref):
    coupling = box_length**2 / (math.pi * points**3)
    shape = (points, 2 * points)

    def squares(index):
        folded = jnp.minimum(index, points - index)
        return folded * folded

    rows = squares(lax.broadcasted_iota(jnp.int32, shape, 0))
    lanes = squares(lax.broadcasted_iota(jnp.int32, shape, 1) % points)

    def step(k, carry):
        total = (rows + lanes + squares(k)).astype(f32)
        value = jnp.where(total > 0.5, coupling / jnp.maximum(total, 1.0), 0.0)
        table_ref[pl.ds(pl.multiple_of(k * points, points), points), :] = value
        return carry

    lax.fori_loop(0, points, step, 0, unroll=4)


def fill_own(points, own_ref, twin_ref):
    width = 2 * points

    def step(y, carry):
        part = own_ref[:, pl.ds(pl.multiple_of(y * width, width), width)].astype(f32)
        twin_ref[:, pl.ds(pl.multiple_of(y * 2 * width, width), 2 * width)] = interleave(part, part)
        return carry

    lax.fori_loop(0, points // 2, step, 0, unroll=4)


def solve_pair(points, first_ref, second_ref, weights, left, right, twin_ref, pair_ref, field_ref, table_ref, sum_ref, between=None):
    width = 2 * points
    pitch = field_ref.shape[0] // points
    group = min(32, points)
    span = min(8, points // 2)

    def into(block, carry):
        values = []
        for k in range(span):
            y = block * span + k
            here = pl.ds(pl.multiple_of(y * width, width), width)
            there = pl.ds(pl.multiple_of(y * 2 * width, width), 2 * width)
            both = interleave(first_ref[:, here].astype(f32), second_ref[:, here].astype(f32))
            pair_ref[:, there] = both
            values.append(both * twin_ref[:, there])
        out = from_left(left, jnp.concatenate(values, axis=1))
        for k in range(2 * span):
            field_ref[pl.ds(2 * span * block + k, points, stride=pitch), :] = out[:, k * width : (k + 1) * width]
        return carry

    lax.fori_loop(0, points // 2 // span, into, 0, unroll=2)

    def middle(x, carry):
        rows = group * points
        base = pl.multiple_of(x * rows, rows)
        value = jnp.concatenate(
            [field_ref[pl.ds(pl.multiple_of((x * group + k) * pitch, 8), points), :] for k in range(group)], axis=1
        )
        value = from_left(left, value)
        value = jnp.concatenate([value[:, k * width : (k + 1) * width] for k in range(group)], axis=0)
        value = from_right(right, value)
        value = from_right(right, value * table_ref[pl.ds(base, rows), :])
        value = jnp.concatenate([value[k * points : (k + 1) * points] for k in range(group)], axis=1)
        value = from_left(left, value)
        for k in range(group):
            field_ref[pl.ds(pl.multiple_of((x * group + k) * pitch, 8), points), :] = value[:, k * width : (k + 1) * width]
        return carry

    lax.fori_loop(0, points // group, middle, 0)

    if between is not None:
        between()

    def out_of(block, carry):
        value = jnp.concatenate(
            [
                field_ref[pl.ds(2 * span * block + k, points, stride=pitch), :]
                for k in range(2 * span)
            ],
            axis=1,
        )
        value = from_left(left, value)
        for k in range(span):
            at = pl.multiple_of((block * span + k) * 2 * width, width)
            there = pl.ds(at, 2 * width)
            sum_ref[:, there] += value[:, 2 * k * width : 2 * (k + 1) * width] * (pair_ref[:, there] * weights)
        return carry

    lax.fori_loop(0, points // 2 // span, out_of, 0, unroll=2)


def lane_weights(points, first, second):
    lane = lax.broadcasted_iota(jnp.int32, (1, 4 * points), 1) % (2 * points)
    return jnp.where(lane < points, first, second)


def folded_sum(points, sum_ref, y, rows=slice(None)):
    width = 2 * points
    at = pl.multiple_of(y * 2 * width, width)
    even, odd = sum_ref[rows, pl.ds(at, width)], sum_ref[rows, pl.ds(at + width, width)]
    even = even + pltpu.roll(even, points, 1)
    odd = odd + pltpu.roll(odd, points, 1)
    return -jnp.where(lower_lanes(even.shape), even, odd)


def work(points, own_ref, visit_ref, weight_ref, left_ref, right_ref, out_ref, twin_ref, pair_ref, field_ref, table_ref, sum_ref):
    width = 2 * points
    fill_kernel(points, table_ref)
    fill_own(points, own_ref, twin_ref)
    sum_ref[...] = jnp.zeros_like(sum_ref)
    left, right = left_ref[...], right_ref[...]

    def pair(p, carry):
        weights = lane_weights(points, weight_ref[0, 2 * p], weight_ref[0, 2 * p + 1])
        solve_pair(
            points, visit_ref.at[2 * p], visit_ref.at[2 * p + 1], weights, left, right,
            twin_ref, pair_ref, field_ref, table_ref, sum_ref,
        )
        return carry

    lax.fori_loop(0, visit_ref.shape[0] // 2, pair, 0)

    def fold(y, carry):
        out_ref[:, pl.ds(pl.multiple_of(y * width, width), width)] = folded_sum(points, sum_ref, y)
        return carry

    lax.fori_loop(0, points // 2, fold, 0, unroll=4)


def act(own, visits, weights):
    points = own.shape[0]
    left, right = cas_tables(points)
    vmem = pl.BlockSpec(memory_space=pltpu.VMEM)
    wide = (points, 2 * points * points)
    tall = (points * points, 2 * points)
    return pl.pallas_call(
        functools.partial(work, points),
        out_shape=jax.ShapeDtypeStruct(own.shape, f32),
        in_specs=[vmem, vmem, pl.BlockSpec(memory_space=pltpu.SMEM), vmem, vmem],
        out_specs=vmem,
        scratch_shapes=[
            pltpu.VMEM(wide, f32),
            pltpu.VMEM(wide, f32),
            pltpu.VMEM((points * (points + 8), 2 * points), f32),
            pltpu.VMEM(tall, f32),
            pltpu.VMEM(wide, f32),
        ],
        compiler_params=pltpu.CompilerParams(vmem_limit_bytes=48 * 2**20),
    )(own, visits, weights, jnp.asarray(left), jnp.asarray(right))


def joint_work(
    points, chips, orb_ref, occ_ref, left_ref, right_ref, out_ref,
    own_ref, visit_ref, twin_ref, pair_ref, field_ref, table_ref, sum_ref, leave_ref, arrive_ref,
    ring_sent, ring_got, core_sent, core_got, lane_sent, lane_got, sum_sent, sum_got,
):
    planes, area = orb_ref.shape
    width = 2 * points
    rank, lane = lax.axis_index("grp"), lax.axis_index("dist")
    core, chip = rank % 2, rank // 2
    place = jnp.where(chip % 2 == 0, chip // 2, chips - 1 - chip // 2)

    def device_at(spot):
        spot = (spot + chips) % chips
        return jnp.where(spot < chips // 2, 2 * spot, 2 * (chips - 1 - spot) + 1) * 2 + core

    ahead = (device_at(place + 1 - 2 * core), lane)
    behind = (device_at(place - 1 + 2 * core), lane)
    sibling = (chip * 2 + 1 - core, lane)
    across = (rank, 1 - lane)
    most = chips // 2
    steps = most - core * (2 * most + 1 - chips)
    source = core == lane

    def rows_of(which):
        side = lane + which - 2 * lane * which
        return pl.ds(pl.multiple_of(side * planes, planes), planes)

    def ring_copy(step, which):
        held = jnp.where(step == 0, 0, 2 * step - 1 + core)
        return pltpu.make_async_remote_copy(
            src_ref=visit_ref.at[held, rows_of(which)],
            dst_ref=visit_ref.at[2 * step + 1 + core, rows_of(which)],
            send_sem=ring_sent.at[step, which],
            recv_sem=ring_got.at[step, which],
            device_id=ahead,
            device_id_type=pl.DeviceIdType.MESH,
        )

    def core_copy(slot, which):
        return pltpu.make_async_remote_copy(
            src_ref=visit_ref.at[slot, rows_of(which)],
            dst_ref=visit_ref.at[slot, rows_of(which)],
            send_sem=core_sent.at[slot, which],
            recv_sem=core_got.at[slot, which],
            device_id=sibling,
            device_id_type=pl.DeviceIdType.MESH,
        )

    lane_copy = pltpu.make_async_remote_copy(
        src_ref=own_ref.at[rows_of(0)],
        dst_ref=own_ref.at[rows_of(0)],
        send_sem=lane_sent,
        recv_sem=lane_got,
        device_id=across,
        device_id_type=pl.DeviceIdType.MESH,
    )
    chunks = sum_sent.shape[0]
    chunk = area // chunks

    def sum_copy(part):
        here = pl.ds(part * chunk, chunk)
        return pltpu.make_async_remote_copy(
            src_ref=leave_ref.at[:, here],
            dst_ref=arrive_ref.at[:, here],
            send_sem=sum_sent.at[part],
            recv_sem=sum_got.at[part],
            device_id=across,
            device_id_type=pl.DeviceIdType.MESH,
        )

    barrier = pltpu.get_barrier_semaphore()
    for other in (ahead, behind, sibling, across):
        pl.semaphore_signal(barrier, inc=1, device_id=other, device_id_type=pl.DeviceIdType.MESH)

    occupied = jnp.full((planes, width), occ_ref[0], f32).astype(bf16)
    own_ref[rows_of(0), pl.ds(0, area)] = orb_ref[...]
    own_ref[rows_of(0), pl.ds(area, width)] = occupied

    @pl.when(source)
    def _():
        visit_ref[0, rows_of(0), :] = own_ref[rows_of(0), :]

    pl.semaphore_wait(barrier, 4)
    lane_copy.start()

    @pl.when(source)
    def _():
        ring_copy(0, 0).start()
        core_copy(0, 0).start()

    fill_kernel(points, table_ref)
    sum_ref[...] = jnp.zeros_like(sum_ref)
    lane_copy.wait_recv()

    @pl.when(source)
    def _():
        visit_ref[0, rows_of(1), :] = own_ref[rows_of(1), :]
        ring_copy(0, 1).start()
        core_copy(0, 1).start()

    @pl.when(jnp.logical_not(source))
    def _():
        for which in range(2):
            core_copy(0, which).wait_recv()
            ring_copy(0, which).start()

    fill_own(points, own_ref, twin_ref)

    def service(step):
        @pl.when(step <= steps)
        def _():
            for which in range(2):
                ring_copy(step - 1, which).wait_recv()

                @pl.when(step < steps)
                def _():
                    ring_copy(step, which).start()

                core_copy(2 * step - 1 + core, which).start()

    service(1)
    left, right = left_ref[...], right_ref[...]
    pairs = chips // 2

    def pair(p, carry):
        @pl.when(core == 1)
        def _():
            for which in range(2):
                core_copy(2 * p + 1, which).wait_recv()

        @pl.when(jnp.logical_and(core == 0, p > 0))
        def _():
            for which in range(2):
                core_copy(2 * p, which).wait_recv()

        near = visit_ref[2 * p, pl.ds(0, 16), pl.ds(area, width)].astype(f32)[:1]
        far = visit_ref[2 * p + 1, pl.ds(0, 16), pl.ds(area, width)].astype(f32)[:1]
        weights = jnp.where(lower_lanes(near.shape), near, far)
        weights = jnp.concatenate([weights, weights], axis=1)
        solve_pair(
            points, visit_ref.at[2 * p], visit_ref.at[2 * p + 1], weights, left, right,
            twin_ref, pair_ref, field_ref, table_ref, sum_ref, lambda: service(p + 2),
        )
        return carry

    lax.fori_loop(0, pairs, pair, 0)

    share = points // 2 // chunks
    for part in range(chunks):

        def fold(y, carry):
            here = pl.ds(pl.multiple_of(y * width, width), width)
            leave_ref[:, here] = folded_sum(points, sum_ref, y, rows_of(1))
            return carry

        lax.fori_loop(part * share, (part + 1) * share, fold, 0, unroll=True)
        sum_copy(part).start()
    for part in range(chunks):
        sum_copy(part).wait_recv()

        def add(y, carry):
            here = pl.ds(pl.multiple_of(y * width, width), width)
            out_ref[:, here] = folded_sum(points, sum_ref, y, rows_of(0)) + arrive_ref[:, here]
            return carry

        lax.fori_loop(part * share, (part + 1) * share, add, 0, unroll=True)

    for part in range(chunks):
        sum_copy(part).wait_send()
    lane_copy.wait_send()
    for which in range(2):

        @pl.when(source)
        def _():
            core_copy(0, which).wait_send()

        for step in range(most):

            @pl.when(step < steps)
            def _():
                ring_copy(step, which).wait_send()
                core_copy(2 * step + 1 + core, which).wait_send()


def joint(orbitals, occupations):
    planes, area = orbitals.shape
    points = planes * lax.axis_size("dist")
    chips = lax.axis_size("grp") // 2
    left, right = cas_tables(points)
    vmem = pl.BlockSpec(memory_space=pltpu.VMEM)
    wide = (points, 2 * points * points)
    tall = (points * points, 2 * points)
    chunks = 4
    dma = pltpu.SemaphoreType.DMA
    return pl.pallas_call(
        functools.partial(joint_work, points, chips),
        out_shape=jax.ShapeDtypeStruct((planes, area), f32),
        in_specs=[vmem, pl.BlockSpec(memory_space=pltpu.SMEM), vmem, vmem],
        out_specs=vmem,
        scratch_shapes=[
            pltpu.VMEM((points, area + 2 * points), bf16),
            pltpu.VMEM((chips, points, area + 2 * points), bf16),
            pltpu.VMEM(wide, f32),
            pltpu.VMEM(wide, f32),
            pltpu.VMEM((points * (points + 8), 2 * points), f32),
            pltpu.VMEM(tall, f32),
            pltpu.VMEM(wide, f32),
            pltpu.VMEM((planes, area), f32),
            pltpu.VMEM((planes, area), f32),
            dma((chips // 2, 2)),
            dma((chips // 2, 2)),
            dma((chips, 2)),
            dma((chips, 2)),
            dma,
            dma,
            dma((chunks,)),
            dma((chunks,)),
        ],
        compiler_params=pltpu.CompilerParams(
            vmem_limit_bytes=48 * 2**20, collective_id=0, has_side_effects=True
        ),
    )(orbitals, occupations.astype(f32), jnp.asarray(left), jnp.asarray(right))


def body(orbitals, occupations):
    lanes = lax.axis_size("dist")
    if lanes == 2 and orbitals.shape[0] == 1 and lax.axis_size("grp") % 4 == 0:
        return joint(orbitals[0], occupations)[None]
    lane = lax.axis_index("dist")
    own = lax.all_gather(orbitals, "dist", axis=1, tiled=True)[0]
    spread = lax.all_gather(orbitals, "grp", axis=0, tiled=True)
    spread_occ = lax.all_gather(occupations, "grp", axis=0, tiled=True)
    orbs, planes, area = spread.shape
    sorted_by_lane = spread.reshape(orbs // lanes, lanes, planes, area).swapaxes(0, 1)
    visits = lax.all_to_all(sorted_by_lane, "dist", split_axis=0, concat_axis=2, tiled=True)[0]
    mine = lax.dynamic_index_in_dim(spread_occ.reshape(orbs // lanes, lanes), lane, 1, keepdims=False)
    partial = act(own, visits, mine.astype(f32)[None])
    return lax.psum_scatter(partial, "dist", scatter_dimension=0, tiled=True)[None]


def solution(mesh):
    in_specs = (P("grp", "dist", None), P("grp"))
    out_specs = P("grp", "dist", None)
    return jax.shard_map(body, mesh=mesh, in_specs=in_specs, out_specs=out_specs, check_vma=False)
```

```python
import functools
import math

import jax
import jax.numpy as jnp
import numpy as np
from jax import lax
from jax.experimental import pallas as pl
from jax.experimental.pallas import tpu as pltpu
from jax.sharding import PartitionSpec as P

box_length = 7.0
bf16, f32 = jnp.bfloat16, jnp.float32


def cas_tables(points):
    position = np.arange(points)
    angle = (position[:, None] * position[None, :] % points) * (2.0 * math.pi / points)
    table = np.cos(angle) + np.sin(angle)
    high = table.astype(bf16)
    low = (table - high.astype(np.float64)).astype(bf16)
    high, low = high.astype(np.float32), low.astype(np.float32)
    left = np.block([[high, high], [low, low]])
    two = np.eye(2, dtype=np.float32)
    wide_high, wide_low = np.kron(two, high), np.kron(two, low)
    right = np.block([[wide_high, wide_low], [wide_high, wide_low]])
    return left.astype(bf16), right.astype(bf16)


def split(value):
    high = value.astype(bf16)
    low = (value - high.astype(f32)).astype(bf16)
    return high, low


def from_left(left, value):
    points = value.shape[0]
    both = jnp.dot(left, jnp.concatenate(split(value), axis=0), preferred_element_type=f32)
    return both[:points] + both[points:]


def from_right(right, value):
    width = value.shape[1]
    both = jnp.dot(jnp.concatenate(split(value), axis=1), right, preferred_element_type=f32)
    return both[:, :width] + both[:, width:]


def lower_lanes(shape):
    return lax.broadcasted_iota(jnp.int32, shape, 1) < shape[1] // 2


def interleave(first, second):
    width = first.shape[1]
    low = lower_lanes(first.shape)
    even = jnp.where(low, first, pltpu.roll(second, width // 2, 1))
    odd = jnp.where(low, pltpu.roll(first, width // 2, 1), second)
    return jnp.concatenate([even, odd], axis=1)


def fill_kernel(points, table_ref):
    coupling = box_length**2 / (math.pi * points**3)
    shape = (points, 2 * points)

    def squares(index):
        folded = jnp.minimum(index, points - index)
        return folded * folded

    rows = squares(lax.broadcasted_iota(jnp.int32, shape, 0))
    lanes = squares(lax.broadcasted_iota(jnp.int32, shape, 1) % points)

    def step(k, carry):
        total = (rows + lanes + squares(k)).astype(f32)
        value = jnp.where(total > 0.5, coupling / jnp.maximum(total, 1.0), 0.0)
        table_ref[pl.ds(pl.multiple_of(k * points, points), points), :] = value
        return carry

    lax.fori_loop(0, points, step, 0, unroll=4)


def fill_own(points, own_ref, twin_ref):
    width = 2 * points

    def step(y, carry):
        part = own_ref[:, pl.ds(pl.multiple_of(y * width, width), width)].astype(f32)
        twin_ref[:, pl.ds(pl.multiple_of(y * 2 * width, width), 2 * width)] = interleave(part, part)
        return carry

    lax.fori_loop(0, points // 2, step, 0, unroll=4)


def solve_pair(points, first_ref, second_ref, weights, left, right, twin_ref, pair_ref, field_ref, table_ref, sum_ref, between=None):
    width = 2 * points
    pitch = field_ref.shape[0] // points
    group = min(32, points)
    span = min(8, points // 2)

    def into(block, carry):
        values = []
        for k in range(span):
            y = block * span + k
            here = pl.ds(pl.multiple_of(y * width, width), width)
            there = pl.ds(pl.multiple_of(y * 2 * width, width), 2 * width)
            both = interleave(first_ref[:, here].astype(f32), second_ref[:, here].astype(f32))
            pair_ref[:, there] = both
            values.append(both * twin_ref[:, there])
        out = from_left(left, jnp.concatenate(values, axis=1))
        for k in range(2 * span):
            field_ref[pl.ds(2 * span * block + k, points, stride=pitch), :] = out[:, k * width : (k + 1) * width]
        return carry

    lax.fori_loop(0, points // 2 // span, into, 0, unroll=2)

    def middle(x, carry):
        rows = group * points
        base = pl.multiple_of(x * rows, rows)
        value = jnp.concatenate(
            [field_ref[pl.ds(pl.multiple_of((x * group + k) * pitch, 8), points), :] for k in range(group)], axis=1
        )
        value = from_left(left, value)
        value = jnp.concatenate([value[:, k * width : (k + 1) * width] for k in range(group)], axis=0)
        value = from_right(right, value)
        value = from_right(right, value * table_ref[pl.ds(base, rows), :])
        value = jnp.concatenate([value[k * points : (k + 1) * points] for k in range(group)], axis=1)
        value = from_left(left, value)
        for k in range(group):
            field_ref[pl.ds(pl.multiple_of((x * group + k) * pitch, 8), points), :] = value[:, k * width : (k + 1) * width]
        return carry

    lax.fori_loop(0, points // group, middle, 0)

    if between is not None:
        between()

    def out_of(block, carry):
        value = jnp.concatenate(
            [
                field_ref[pl.ds(2 * span * block + k, points, stride=pitch), :]
                for k in range(2 * span)
            ],
            axis=1,
        )
        value = from_left(left, value)
        for k in range(span):
            at = pl.multiple_of((block * span + k) * 2 * width, width)
            there = pl.ds(at, 2 * width)
            sum_ref[:, there] += value[:, 2 * k * width : 2 * (k + 1) * width] * (pair_ref[:, there] * weights)
        return carry

    lax.fori_loop(0, points // 2 // span, out_of, 0, unroll=2)


def lane_weights(points, first, second):
    lane = lax.broadcasted_iota(jnp.int32, (1, 4 * points), 1) % (2 * points)
    return jnp.where(lane < points, first, second)


def folded_sum(points, sum_ref, y, rows=slice(None)):
    width = 2 * points
    at = pl.multiple_of(y * 2 * width, width)
    even, odd = sum_ref[rows, pl.ds(at, width)], sum_ref[rows, pl.ds(at + width, width)]
    even = even + pltpu.roll(even, points, 1)
    odd = odd + pltpu.roll(odd, points, 1)
    return -jnp.where(lower_lanes(even.shape), even, odd)


def work(points, own_ref, visit_ref, weight_ref, left_ref, right_ref, out_ref, twin_ref, pair_ref, field_ref, table_ref, sum_ref):
    width = 2 * points
    fill_kernel(points, table_ref)
    fill_own(points, own_ref, twin_ref)
    sum_ref[...] = jnp.zeros_like(sum_ref)
    left, right = left_ref[...], right_ref[...]

    def pair(p, carry):
        weights = lane_weights(points, weight_ref[0, 2 * p], weight_ref[0, 2 * p + 1])
        solve_pair(
            points, visit_ref.at[2 * p], visit_ref.at[2 * p + 1], weights, left, right,
            twin_ref, pair_ref, field_ref, table_ref, sum_ref,
        )
        return carry

    lax.fori_loop(0, visit_ref.shape[0] // 2, pair, 0)

    def fold(y, carry):
        out_ref[:, pl.ds(pl.multiple_of(y * width, width), width)] = folded_sum(points, sum_ref, y)
        return carry

    lax.fori_loop(0, points // 2, fold, 0, unroll=4)


def act(own, visits, weights):
    points = own.shape[0]
    left, right = cas_tables(points)
    vmem = pl.BlockSpec(memory_space=pltpu.VMEM)
    wide = (points, 2 * points * points)
    tall = (points * points, 2 * points)
    return pl.pallas_call(
        functools.partial(work, points),
        out_shape=jax.ShapeDtypeStruct(own.shape, f32),
        in_specs=[vmem, vmem, pl.BlockSpec(memory_space=pltpu.SMEM), vmem, vmem],
        out_specs=vmem,
        scratch_shapes=[
            pltpu.VMEM(wide, f32),
            pltpu.VMEM(wide, f32),
            pltpu.VMEM((points * (points + 8), 2 * points), f32),
            pltpu.VMEM(tall, f32),
            pltpu.VMEM(wide, f32),
        ],
        compiler_params=pltpu.CompilerParams(vmem_limit_bytes=48 * 2**20),
    )(own, visits, weights, jnp.asarray(left), jnp.asarray(right))


def joint_work(
    points, chips, orb_ref, occ_ref, left_hbm, right_hbm, out_ref, left_ref, right_ref,
    own_ref, visit_ref, twin_ref, pair_ref, field_ref, table_ref, sum_ref, leave_ref, arrive_ref,
    ring_sent, ring_got, core_sent, core_got, lane_sent, lane_got, sum_sent, sum_got, load_sems,
):
    planes, area = orb_ref.shape
    width = 2 * points
    rank, lane = lax.axis_index("grp"), lax.axis_index("dist")
    core, chip = rank % 2, rank // 2
    place = jnp.where(chip % 2 == 0, chip // 2, chips - 1 - chip // 2)

    def device_at(spot):
        spot = (spot + chips) % chips
        return jnp.where(spot < chips // 2, 2 * spot, 2 * (chips - 1 - spot) + 1) * 2 + core

    ahead = (device_at(place + 1 - 2 * core), lane)
    behind = (device_at(place - 1 + 2 * core), lane)
    sibling = (chip * 2 + 1 - core, lane)
    across = (rank, 1 - lane)
    most = chips // 2
    source = core == lane

    def rows_of(which):
        side = lane + which - 2 * lane * which
        return pl.ds(pl.multiple_of(side * planes, planes), planes)

    def slot_after(step):
        return jnp.minimum(2 * step + 1 + core, chips - 1)

    def is_sent(step, which):
        return jnp.logical_or(step < most - 1, jnp.logical_and(step == most - 1, core == which))

    def ring_copy(step, which):
        held = jnp.where(step == 0, 0, 2 * step - 1 + core)
        return pltpu.make_async_remote_copy(
            src_ref=visit_ref.at[held, rows_of(which)],
            dst_ref=visit_ref.at[slot_after(step), rows_of(which)],
            send_sem=ring_sent.at[step, which],
            recv_sem=ring_got.at[step, which],
            device_id=ahead,
            device_id_type=pl.DeviceIdType.MESH,
        )

    def core_copy(slot, which):
        return pltpu.make_async_remote_copy(
            src_ref=visit_ref.at[slot, rows_of(which)],
            dst_ref=visit_ref.at[slot, rows_of(which)],
            send_sem=core_sent.at[slot, which],
            recv_sem=core_got.at[slot, which],
            device_id=sibling,
            device_id_type=pl.DeviceIdType.MESH,
        )

    lane_copy = pltpu.make_async_remote_copy(
        src_ref=own_ref.at[rows_of(0)],
        dst_ref=own_ref.at[rows_of(0)],
        send_sem=lane_sent,
        recv_sem=lane_got,
        device_id=across,
        device_id_type=pl.DeviceIdType.MESH,
    )
    chunks = sum_sent.shape[0]
    chunk = area // chunks

    def sum_copy(part):
        here = pl.ds(part * chunk, chunk)
        return pltpu.make_async_remote_copy(
            src_ref=leave_ref.at[:, here],
            dst_ref=arrive_ref.at[:, here],
            send_sem=sum_sent.at[part],
            recv_sem=sum_got.at[part],
            device_id=across,
            device_id_type=pl.DeviceIdType.MESH,
        )

    def service(step, which):
        @pl.when(is_sent(step - 1, which))
        def _():
            ring_copy(step - 1, which).wait_recv()

            @pl.when(is_sent(step, which))
            def _():
                ring_copy(step, which).start()

            core_copy(slot_after(step - 1), which).start()

    barrier = pltpu.get_barrier_semaphore()
    for other in (ahead, behind, sibling, across):
        pl.semaphore_signal(barrier, inc=1, device_id=other, device_id_type=pl.DeviceIdType.MESH)

    load_own = pltpu.make_async_copy(orb_ref, own_ref.at[rows_of(0), pl.ds(0, area)], load_sems.at[0])
    load_left = pltpu.make_async_copy(left_hbm, left_ref, load_sems.at[1])
    load_right = pltpu.make_async_copy(right_hbm, right_ref, load_sems.at[2])
    load_own.start()
    load_left.start()
    load_right.start()
    own_ref[rows_of(0), pl.ds(area, width)] = jnp.full((planes, width), occ_ref[0], f32).astype(bf16)
    load_own.wait()

    @pl.when(source)
    def _():
        visit_ref[0, rows_of(0), :] = own_ref[rows_of(0), :]

    pl.semaphore_wait(barrier, 4)

    @pl.when(source)
    def _():
        core_copy(0, 0).start()
        ring_copy(0, 0).start()

    @pl.when(jnp.logical_not(source))
    def _():
        lane_copy.start()
        core_copy(0, 0).wait_recv()
        ring_copy(0, 0).start()

    fill_kernel(points, table_ref)
    sum_ref[...] = jnp.zeros_like(sum_ref)
    load_left.wait()
    load_right.wait()

    @pl.when(source)
    def _():
        lane_copy.wait_recv()
        visit_ref[0, rows_of(1), :] = own_ref[rows_of(1), :]
        core_copy(0, 1).start()
        ring_copy(0, 1).start()
        lane_copy.start()

    @pl.when(jnp.logical_not(source))
    def _():
        core_copy(0, 1).wait_recv()
        ring_copy(0, 1).start()

    service(1, 0)

    @pl.when(jnp.logical_not(source))
    def _():
        lane_copy.wait_recv()

    fill_own(points, own_ref, twin_ref)
    service(1, 1)
    left, right = left_ref[...], right_ref[...]
    pairs = chips // 2

    def pair(p, carry):
        for which in range(2):

            @pl.when(jnp.logical_and(core == 0, p > 0))
            def _():
                core_copy(2 * p, which).wait_recv()

            @pl.when(jnp.where(p < pairs - 1, core == 1, core != which))
            def _():
                core_copy(2 * p + 1, which).wait_recv()

        near = visit_ref[2 * p, pl.ds(0, 16), pl.ds(area, width)].astype(f32)[:1]
        far = visit_ref[2 * p + 1, pl.ds(0, 16), pl.ds(area, width)].astype(f32)[:1]
        weights = jnp.where(lower_lanes(near.shape), near, far)
        weights = jnp.concatenate([weights, weights], axis=1)
        solve_pair(
            points, visit_ref.at[2 * p], visit_ref.at[2 * p + 1], weights, left, right,
            twin_ref, pair_ref, field_ref, table_ref, sum_ref, lambda: service(p + 2, 0),
        )
        service(p + 2, 1)
        return carry

    lax.fori_loop(0, pairs, pair, 0)

    share = points // 2 // chunks
    for part in range(chunks):

        def fold(y, carry):
            here = pl.ds(pl.multiple_of(y * width, width), width)
            leave_ref[:, here] = folded_sum(points, sum_ref, y, rows_of(1))
            return carry

        lax.fori_loop(part * share, (part + 1) * share, fold, 0, unroll=True)
        sum_copy(part).start()
    for part in range(chunks):
        sum_copy(part).wait_recv()

        def add(y, carry):
            here = pl.ds(pl.multiple_of(y * width, width), width)
            out_ref[:, here] = folded_sum(points, sum_ref, y, rows_of(0)) + arrive_ref[:, here]
            return carry

        lax.fori_loop(part * share, (part + 1) * share, add, 0, unroll=True)

    for part in range(chunks):
        sum_copy(part).wait_send()
    lane_copy.wait_send()
    for which in range(2):

        @pl.when(source)
        def _():
            core_copy(0, which).wait_send()

        for step in range(most):

            @pl.when(is_sent(step, which))
            def _():
                ring_copy(step, which).wait_send()
                core_copy(slot_after(step), which).wait_send()


def joint(orbitals, occupations):
    planes, area = orbitals.shape
    points = planes * lax.axis_size("dist")
    chips = lax.axis_size("grp") // 2
    left, right = cas_tables(points)
    vmem = pl.BlockSpec(memory_space=pltpu.VMEM)
    hbm = pl.BlockSpec(memory_space=pl.ANY)
    wide = (points, 2 * points * points)
    tall = (points * points, 2 * points)
    chunks = 4
    dma = pltpu.SemaphoreType.DMA
    return pl.pallas_call(
        functools.partial(joint_work, points, chips),
        out_shape=jax.ShapeDtypeStruct((planes, area), f32),
        in_specs=[hbm, pl.BlockSpec(memory_space=pltpu.SMEM), hbm, hbm],
        out_specs=vmem,
        scratch_shapes=[
            pltpu.VMEM(left.shape, bf16),
            pltpu.VMEM(right.shape, bf16),
            pltpu.VMEM((points, area + 2 * points), bf16),
            pltpu.VMEM((chips, points, area + 2 * points), bf16),
            pltpu.VMEM(wide, f32),
            pltpu.VMEM(wide, f32),
            pltpu.VMEM((points * (points + 8), 2 * points), f32),
            pltpu.VMEM(tall, f32),
            pltpu.VMEM(wide, f32),
            pltpu.VMEM((planes, area), f32),
            pltpu.VMEM((planes, area), f32),
            dma((chips // 2, 2)),
            dma((chips // 2, 2)),
            dma((chips, 2)),
            dma((chips, 2)),
            dma,
            dma,
            dma((chunks,)),
            dma((chunks,)),
            dma((3,)),
        ],
        compiler_params=pltpu.CompilerParams(
            vmem_limit_bytes=48 * 2**20, collective_id=0, has_side_effects=True
        ),
    )(orbitals, occupations.astype(f32), jnp.asarray(left), jnp.asarray(right))


def body(orbitals, occupations):
    lanes = lax.axis_size("dist")
    if lanes == 2 and orbitals.shape[0] == 1 and lax.axis_size("grp") % 4 == 0 and lax.axis_size("grp") > 4:
        return joint(orbitals[0], occupations)[None]
    lane = lax.axis_index("dist")
    own = lax.all_gather(orbitals, "dist", axis=1, tiled=True)[0]
    spread = lax.all_gather(orbitals, "grp", axis=0, tiled=True)
    spread_occ = lax.all_gather(occupations, "grp", axis=0, tiled=True)
    orbs, planes, area = spread.shape
    sorted_by_lane = spread.reshape(orbs // lanes, lanes, planes, area).swapaxes(0, 1)
    visits = lax.all_to_all(sorted_by_lane, "dist", split_axis=0, concat_axis=2, tiled=True)[0]
    mine = lax.dynamic_index_in_dim(spread_occ.reshape(orbs // lanes, lanes), lane, 1, keepdims=False)
    partial = act(own, visits, mine.astype(f32)[None])
    return lax.psum_scatter(partial, "dist", scatter_dimension=0, tiled=True)[None]


def solution(mesh):
    in_specs = (P("grp", "dist", None), P("grp"))
    out_specs = P("grp", "dist", None)
    return jax.shard_map(body, mesh=mesh, in_specs=in_specs, out_specs=out_specs, check_vma=False)
```

```python
import functools
import math

import jax
import jax.numpy as jnp
import numpy as np
from jax import lax
from jax.experimental import pallas as pl
from jax.experimental.pallas import tpu as pltpu
from jax.sharding import PartitionSpec as P

box_length = 7.0
bf16, f32 = jnp.bfloat16, jnp.float32


def cas_tables(points):
    position = np.arange(points)
    angle = (position[:, None] * position[None, :] % points) * (2.0 * math.pi / points)
    table = np.cos(angle) + np.sin(angle)
    high = table.astype(bf16)
    low = (table - high.astype(np.float64)).astype(bf16)
    high, low = high.astype(np.float32), low.astype(np.float32)
    left = np.block([[high, high], [low, low]])
    two = np.eye(2, dtype=np.float32)
    wide_high, wide_low = np.kron(two, high), np.kron(two, low)
    right = np.block([[wide_high, wide_low], [wide_high, wide_low]])
    return left.astype(bf16), right.astype(bf16)


def split(value):
    high = value.astype(bf16)
    low = (value - high.astype(f32)).astype(bf16)
    return high, low


def from_left(left, value):
    points = value.shape[0]
    both = jnp.dot(left, jnp.concatenate(split(value), axis=0), preferred_element_type=f32)
    return both[:points] + both[points:]


def from_right(right, value):
    width = value.shape[1]
    both = jnp.dot(jnp.concatenate(split(value), axis=1), right, preferred_element_type=f32)
    return both[:, :width] + both[:, width:]


def lower_lanes(shape):
    return lax.broadcasted_iota(jnp.int32, shape, 1) < shape[1] // 2


def interleave(first, second):
    width = first.shape[1]
    low = lower_lanes(first.shape)
    even = jnp.where(low, first, pltpu.roll(second, width // 2, 1))
    odd = jnp.where(low, pltpu.roll(first, width // 2, 1), second)
    return jnp.concatenate([even, odd], axis=1)


def fill_kernel(points, table_ref):
    coupling = box_length**2 / (math.pi * points**3)
    shape = (points, 2 * points)

    def squares(index):
        folded = jnp.minimum(index, points - index)
        return folded * folded

    rows = squares(lax.broadcasted_iota(jnp.int32, shape, 0))
    lanes = squares(lax.broadcasted_iota(jnp.int32, shape, 1) % points)

    def step(k, carry):
        total = (rows + lanes + squares(k)).astype(f32)
        value = jnp.where(total > 0.5, coupling / jnp.maximum(total, 1.0), 0.0)
        table_ref[pl.ds(pl.multiple_of(k * points, points), points), :] = value
        return carry

    lax.fori_loop(0, points, step, 0, unroll=4)


def fill_own(points, own_ref, twin_ref):
    width = 2 * points

    def step(y, carry):
        part = own_ref[:, pl.ds(pl.multiple_of(y * width, width), width)].astype(f32)
        twin_ref[:, pl.ds(pl.multiple_of(y * 2 * width, width), 2 * width)] = interleave(part, part)
        return carry

    lax.fori_loop(0, points // 2, step, 0, unroll=4)


def solve_pair(points, first_ref, second_ref, weights, left, right, twin_ref, pair_ref, field_ref, table_ref, sum_ref, between=None, after=None):
    width = 2 * points
    pitch = field_ref.shape[0] // points
    group = min(32, points)
    span = min(8, points // 2)

    def into(block, carry):
        values = []
        for k in range(span):
            y = block * span + k
            here = pl.ds(pl.multiple_of(y * width, width), width)
            there = pl.ds(pl.multiple_of(y * 2 * width, width), 2 * width)
            both = interleave(first_ref[:, here].astype(f32), second_ref[:, here].astype(f32))
            pair_ref[:, there] = both
            values.append(both * twin_ref[:, there])
        out = from_left(left, jnp.concatenate(values, axis=1))
        for k in range(2 * span):
            field_ref[pl.ds(2 * span * block + k, points, stride=pitch), :] = out[:, k * width : (k + 1) * width]
        return carry

    lax.fori_loop(0, points // 2 // span, into, 0, unroll=2)

    def middle(x, carry):
        rows = group * points
        base = pl.multiple_of(x * rows, rows)
        value = jnp.concatenate(
            [field_ref[pl.ds(pl.multiple_of((x * group + k) * pitch, 8), points), :] for k in range(group)], axis=1
        )
        value = from_left(left, value)
        value = jnp.concatenate([value[:, k * width : (k + 1) * width] for k in range(group)], axis=0)
        value = from_right(right, value)
        value = from_right(right, value * table_ref[pl.ds(base, rows), :])
        value = jnp.concatenate([value[k * points : (k + 1) * points] for k in range(group)], axis=1)
        value = from_left(left, value)
        for k in range(group):
            field_ref[pl.ds(pl.multiple_of((x * group + k) * pitch, 8), points), :] = value[:, k * width : (k + 1) * width]
        return carry

    lax.fori_loop(0, points // group, middle, 0)

    if between is not None:
        between()

    def out_of(block, carry):
        value = jnp.concatenate(
            [
                field_ref[pl.ds(2 * span * block + k, points, stride=pitch), :]
                for k in range(2 * span)
            ],
            axis=1,
        )
        value = from_left(left, value)
        for k in range(span):
            at = pl.multiple_of((block * span + k) * 2 * width, width)
            there = pl.ds(at, 2 * width)
            sum_ref[:, there] += value[:, 2 * k * width : 2 * (k + 1) * width] * (pair_ref[:, there] * weights)
        if after is not None:
            after(block)
        return carry

    lax.fori_loop(0, points // 2 // span, out_of, 0, unroll=2)


def lane_weights(points, first, second):
    lane = lax.broadcasted_iota(jnp.int32, (1, 4 * points), 1) % (2 * points)
    return jnp.where(lane < points, first, second)


def folded_sum(points, sum_ref, y, rows=slice(None)):
    width = 2 * points
    at = pl.multiple_of(y * 2 * width, width)
    even, odd = sum_ref[rows, pl.ds(at, width)], sum_ref[rows, pl.ds(at + width, width)]
    even = even + pltpu.roll(even, points, 1)
    odd = odd + pltpu.roll(odd, points, 1)
    return -jnp.where(lower_lanes(even.shape), even, odd)


def work(points, own_ref, visit_ref, weight_ref, left_ref, right_ref, out_ref, twin_ref, pair_ref, field_ref, table_ref, sum_ref):
    width = 2 * points
    fill_kernel(points, table_ref)
    fill_own(points, own_ref, twin_ref)
    sum_ref[...] = jnp.zeros_like(sum_ref)
    left, right = left_ref[...], right_ref[...]

    def pair(p, carry):
        weights = lane_weights(points, weight_ref[0, 2 * p], weight_ref[0, 2 * p + 1])
        solve_pair(
            points, visit_ref.at[2 * p], visit_ref.at[2 * p + 1], weights, left, right,
            twin_ref, pair_ref, field_ref, table_ref, sum_ref,
        )
        return carry

    lax.fori_loop(0, visit_ref.shape[0] // 2, pair, 0)

    def fold(y, carry):
        out_ref[:, pl.ds(pl.multiple_of(y * width, width), width)] = folded_sum(points, sum_ref, y)
        return carry

    lax.fori_loop(0, points // 2, fold, 0, unroll=4)


def act(own, visits, weights):
    points = own.shape[0]
    left, right = cas_tables(points)
    vmem = pl.BlockSpec(memory_space=pltpu.VMEM)
    wide = (points, 2 * points * points)
    tall = (points * points, 2 * points)
    return pl.pallas_call(
        functools.partial(work, points),
        out_shape=jax.ShapeDtypeStruct(own.shape, f32),
        in_specs=[vmem, vmem, pl.BlockSpec(memory_space=pltpu.SMEM), vmem, vmem],
        out_specs=vmem,
        scratch_shapes=[
            pltpu.VMEM(wide, f32),
            pltpu.VMEM(wide, f32),
            pltpu.VMEM((points * (points + 8), 2 * points), f32),
            pltpu.VMEM(tall, f32),
            pltpu.VMEM(wide, f32),
        ],
        compiler_params=pltpu.CompilerParams(vmem_limit_bytes=48 * 2**20),
    )(own, visits, weights, jnp.asarray(left), jnp.asarray(right))


def joint_work(
    points, chips, orb_ref, occ_ref, left_hbm, right_hbm, out_ref, left_ref, right_ref,
    own_ref, visit_ref, twin_ref, pair_ref, field_ref, table_ref, sum_ref, leave_ref, arrive_ref,
    ring_sent, ring_got, core_sent, core_got, lane_sent, lane_got, sum_sent, sum_got, load_sems,
):
    planes, area = orb_ref.shape
    width = 2 * points
    rank, lane = lax.axis_index("grp"), lax.axis_index("dist")
    core, chip = rank % 2, rank // 2
    place = jnp.where(chip % 2 == 0, chip // 2, chips - 1 - chip // 2)

    def device_at(spot):
        spot = (spot + chips) % chips
        return jnp.where(spot < chips // 2, 2 * spot, 2 * (chips - 1 - spot) + 1) * 2 + core

    ahead = (device_at(place + 1 - 2 * core), lane)
    behind = (device_at(place - 1 + 2 * core), lane)
    sibling = (chip * 2 + 1 - core, lane)
    across = (rank, 1 - lane)
    most = chips // 2
    source = core == lane

    def rows_of(which):
        side = lane + which - 2 * lane * which
        return pl.ds(pl.multiple_of(side * planes, planes), planes)

    def slot_after(step):
        return jnp.minimum(2 * step + 1 + core, chips - 1)

    def is_sent(step, which):
        return jnp.logical_or(step < most - 1, jnp.logical_and(step == most - 1, core == which))

    def ring_copy(step, which):
        held = jnp.where(step == 0, 0, 2 * step - 1 + core)
        return pltpu.make_async_remote_copy(
            src_ref=visit_ref.at[held, rows_of(which)],
            dst_ref=visit_ref.at[slot_after(step), rows_of(which)],
            send_sem=ring_sent.at[step, which],
            recv_sem=ring_got.at[step, which],
            device_id=ahead,
            device_id_type=pl.DeviceIdType.MESH,
        )

    def core_copy(slot, which):
        return pltpu.make_async_remote_copy(
            src_ref=visit_ref.at[slot, rows_of(which)],
            dst_ref=visit_ref.at[slot, rows_of(which)],
            send_sem=core_sent.at[slot, which],
            recv_sem=core_got.at[slot, which],
            device_id=sibling,
            device_id_type=pl.DeviceIdType.MESH,
        )

    lane_copy = pltpu.make_async_remote_copy(
        src_ref=own_ref.at[rows_of(0)],
        dst_ref=own_ref.at[rows_of(0)],
        send_sem=lane_sent,
        recv_sem=lane_got,
        device_id=across,
        device_id_type=pl.DeviceIdType.MESH,
    )
    chunks = sum_sent.shape[0]
    chunk = area // chunks

    def sum_copy(part):
        here = pl.ds(pl.multiple_of(part * chunk, chunk), chunk)
        return pltpu.make_async_remote_copy(
            src_ref=leave_ref.at[:, here],
            dst_ref=arrive_ref.at[:, here],
            send_sem=sum_sent.at[part],
            recv_sem=sum_got.at[part],
            device_id=across,
            device_id_type=pl.DeviceIdType.MESH,
        )

    def service(step, which):
        @pl.when(is_sent(step - 1, which))
        def _():
            ring_copy(step - 1, which).wait_recv()

            @pl.when(is_sent(step, which))
            def _():
                ring_copy(step, which).start()

            core_copy(slot_after(step - 1), which).start()

    barrier = pltpu.get_barrier_semaphore()
    for other in (ahead, behind, sibling, across):
        pl.semaphore_signal(barrier, inc=1, device_id=other, device_id_type=pl.DeviceIdType.MESH)

    load_own = pltpu.make_async_copy(orb_ref, own_ref.at[rows_of(0), pl.ds(0, area)], load_sems.at[0])
    load_left = pltpu.make_async_copy(left_hbm, left_ref, load_sems.at[1])
    load_right = pltpu.make_async_copy(right_hbm, right_ref, load_sems.at[2])
    load_own.start()
    load_left.start()
    load_right.start()
    own_ref[rows_of(0), pl.ds(area, width)] = jnp.full((planes, width), occ_ref[0], f32).astype(bf16)
    load_own.wait()

    @pl.when(source)
    def _():
        visit_ref[0, rows_of(0), :] = own_ref[rows_of(0), :]

    pl.semaphore_wait(barrier, 4)

    @pl.when(source)
    def _():
        core_copy(0, 0).start()
        ring_copy(0, 0).start()

    @pl.when(jnp.logical_not(source))
    def _():
        lane_copy.start()
        core_copy(0, 0).wait_recv()
        ring_copy(0, 0).start()

    fill_kernel(points, table_ref)
    sum_ref[...] = jnp.zeros_like(sum_ref)
    load_left.wait()
    load_right.wait()

    @pl.when(source)
    def _():
        lane_copy.wait_recv()
        visit_ref[0, rows_of(1), :] = own_ref[rows_of(1), :]
        core_copy(0, 1).start()
        ring_copy(0, 1).start()
        lane_copy.start()

    @pl.when(jnp.logical_not(source))
    def _():
        core_copy(0, 1).wait_recv()
        ring_copy(0, 1).start()

    service(1, 0)

    @pl.when(jnp.logical_not(source))
    def _():
        lane_copy.wait_recv()

    fill_own(points, own_ref, twin_ref)
    service(1, 1)
    left, right = left_ref[...], right_ref[...]
    pairs = chips // 2

    share = points // 2 // chunks

    def pair(p, carry):
        def send_sums(part):
            @pl.when(p == pairs - 1)
            def _():
                for k in range(share):
                    y = part * share + k
                    here = pl.ds(pl.multiple_of(y * width, width), width)
                    leave_ref[:, here] = folded_sum(points, sum_ref, y, rows_of(1))
                sum_copy(part).start()

        for which in range(2):

            @pl.when(jnp.logical_and(core == 0, p > 0))
            def _():
                core_copy(2 * p, which).wait_recv()

            @pl.when(jnp.where(p < pairs - 1, core == 1, core != which))
            def _():
                core_copy(2 * p + 1, which).wait_recv()

        near = visit_ref[2 * p, pl.ds(0, 16), pl.ds(area, width)].astype(f32)[:1]
        far = visit_ref[2 * p + 1, pl.ds(0, 16), pl.ds(area, width)].astype(f32)[:1]
        weights = jnp.where(lower_lanes(near.shape), near, far)
        weights = jnp.concatenate([weights, weights], axis=1)
        solve_pair(
            points, visit_ref.at[2 * p], visit_ref.at[2 * p + 1], weights, left, right,
            twin_ref, pair_ref, field_ref, table_ref, sum_ref, lambda: service(p + 2, 0), send_sums,
        )
        service(p + 2, 1)
        return carry

    lax.fori_loop(0, pairs, pair, 0)

    for part in range(chunks):
        sum_copy(part).wait_recv()

        def add(y, carry):
            here = pl.ds(pl.multiple_of(y * width, width), width)
            out_ref[:, here] = folded_sum(points, sum_ref, y, rows_of(0)) + arrive_ref[:, here]
            return carry

        lax.fori_loop(part * share, (part + 1) * share, add, 0, unroll=True)

    for part in range(chunks):
        sum_copy(part).wait_send()
    lane_copy.wait_send()
    for which in range(2):

        @pl.when(source)
        def _():
            core_copy(0, which).wait_send()

        for step in range(most):

            @pl.when(is_sent(step, which))
            def _():
                ring_copy(step, which).wait_send()
                core_copy(slot_after(step), which).wait_send()


def joint(orbitals, occupations):
    planes, area = orbitals.shape
    points = planes * lax.axis_size("dist")
    chips = lax.axis_size("grp") // 2
    left, right = cas_tables(points)
    vmem = pl.BlockSpec(memory_space=pltpu.VMEM)
    hbm = pl.BlockSpec(memory_space=pl.ANY)
    wide = (points, 2 * points * points)
    tall = (points * points, 2 * points)
    chunks = points // 2 // min(8, points // 2)
    dma = pltpu.SemaphoreType.DMA
    return pl.pallas_call(
        functools.partial(joint_work, points, chips),
        out_shape=jax.ShapeDtypeStruct((planes, area), f32),
        in_specs=[hbm, pl.BlockSpec(memory_space=pltpu.SMEM), hbm, hbm],
        out_specs=vmem,
        scratch_shapes=[
            pltpu.VMEM(left.shape, bf16),
            pltpu.VMEM(right.shape, bf16),
            pltpu.VMEM((points, area + 2 * points), bf16),
            pltpu.VMEM((chips, points, area + 2 * points), bf16),
            pltpu.VMEM(wide, f32),
            pltpu.VMEM(wide, f32),
            pltpu.VMEM((points * (points + 8), 2 * points), f32),
            pltpu.VMEM(tall, f32),
            pltpu.VMEM(wide, f32),
            pltpu.VMEM((planes, area), f32),
            pltpu.VMEM((planes, area), f32),
            dma((chips // 2, 2)),
            dma((chips // 2, 2)),
            dma((chips, 2)),
            dma((chips, 2)),
            dma,
            dma,
            dma((chunks,)),
            dma((chunks,)),
            dma((3,)),
        ],
        compiler_params=pltpu.CompilerParams(
            vmem_limit_bytes=48 * 2**20, collective_id=0, has_side_effects=True
        ),
    )(orbitals, occupations.astype(f32), jnp.asarray(left), jnp.asarray(right))


def body(orbitals, occupations):
    lanes = lax.axis_size("dist")
    if lanes == 2 and orbitals.shape[0] == 1 and lax.axis_size("grp") % 4 == 0 and lax.axis_size("grp") > 4:
        return joint(orbitals[0], occupations)[None]
    lane = lax.axis_index("dist")
    own = lax.all_gather(orbitals, "dist", axis=1, tiled=True)[0]
    spread = lax.all_gather(orbitals, "grp", axis=0, tiled=True)
    spread_occ = lax.all_gather(occupations, "grp", axis=0, tiled=True)
    orbs, planes, area = spread.shape
    sorted_by_lane = spread.reshape(orbs // lanes, lanes, planes, area).swapaxes(0, 1)
    visits = lax.all_to_all(sorted_by_lane, "dist", split_axis=0, concat_axis=2, tiled=True)[0]
    mine = lax.dynamic_index_in_dim(spread_occ.reshape(orbs // lanes, lanes), lane, 1, keepdims=False)
    partial = act(own, visits, mine.astype(f32)[None])
    return lax.psum_scatter(partial, "dist", scatter_dimension=0, tiled=True)[None]


def solution(mesh):
    in_specs = (P("grp", "dist", None), P("grp"))
    out_specs = P("grp", "dist", None)
    return jax.shard_map(body, mesh=mesh, in_specs=in_specs, out_specs=out_specs, check_vma=False)
```
